128 devices in a mesh: row: 8 (over x_hi, z), col: 16 (over x_lo, y, core).
Axes of the slice: x: 4 (x_hi: 2, x_lo: 2; x = x_hi * 2 + x_lo), y: 4, z: 4, core: 2. Of those that a mesh axis runs over, the one named last changes fastest.
Arguments:
- three_index: bfloat16 [16384, 4096], P(('row', 'col')), may hold values from -0.59765625 to 0.59765625
- occ_index: int32 [4096], replicated, may hold values from 0 to 999
- vir_index: int32 [4096], replicated, may hold values from 0 to 3999
- occ_energy: float32 [1000], replicated, may hold values from -1.5 to -0.3
- vir_energy: float32 [4000], replicated, may hold values from 0.1 to 3
- frequency: float32 [1], replicated, may hold values from 0.3 to 2
Outputs:
- polar: float32 [16384, 8, 16, 128], P('row', None, 'col')
The draws below stay inside these ranges and needn't reach their ends.
All inputs are finite; a program needn't handle non-finite values.
Results may differ from the reference program's by a relative error of at most 0.0026.
Values may be sent and summed in bfloat16 or wider, within the bound.
No kernel may reach another device: no remote copies, remote signals or barrier semaphores. Data moves between devices by JAX's collectives and lax.ppermute only.
A program may use at most 128 MiB of HBM per device.

```python
import jax
import jax.numpy as jnp
from jax import lax

AUX_DEV = 128
NPAIR = 4096
NOCC = 1000
NVIR = 4000
NAUX = 16384
N_ROW = 8
N_COL = 16


def with_ends(drawn, stream_key, low, high):
    index_at = [jax.random.randint(jax.random.fold_in(stream_key, axis), (), 0, length) for axis, length in enumerate(drawn.shape)]
    longest = drawn.shape.index(max(drawn.shape))
    neighbour = index_at[:longest] + [(index_at[longest] + 1) % drawn.shape[longest]] + index_at[longest + 1:]
    return drawn.at[tuple(index_at)].set(low).at[tuple(neighbour)].set(high)


def levels(rng, dims, shards, low, high):
    def one(position, parts):
        steps = jax.random.uniform(jax.random.fold_in(jax.random.fold_in(rng, 6), position), (parts,), jnp.float32, low / len(shards), high / len(shards))
        return jnp.repeat(jnp.exp(steps), dims[position] // parts).reshape((-1,) + (1,) * (len(dims) - position - 1))

    factor_of = one(*shards[0])
    for cut in shards[1:]:
        factor_of = factor_of * one(*cut)
    return factor_of


def gaussian(stream_key, extent, width, reach, pieces=(), kind=jnp.bfloat16):
    entries = jax.random.normal(stream_key, extent, jnp.float32) * width
    if len(pieces) > 0:
        entries = levels(stream_key, extent, pieces, -0.22, 0.18) * entries
    return jnp.clip(entries, min=-reach, max=reach).astype(kind)


def setup_inputs(seed: int = 0) -> dict:
    splits = jax.random.split(jax.random.key(seed), 7)
    return {
        "three_index": gaussian(splits[0], (NAUX, NPAIR), 0.1, 0.59765625, ((0, 128),)),
        "occ_index": with_ends(jax.random.randint(splits[1], (NPAIR,), 0, NOCC), jax.random.fold_in(splits[1], 1), 0, NOCC - 1).astype(jnp.int32),
        "vir_index": with_ends(jax.random.randint(splits[2], (NPAIR,), 0, NVIR), jax.random.fold_in(splits[2], 1), 0, NVIR - 1).astype(jnp.int32),
        "occ_energy": jnp.clip(jax.random.uniform(splits[3], (NOCC,), jnp.float32, -1.5, -0.3), -1.5, -0.3),
        "vir_energy": jnp.clip(jax.random.uniform(splits[4], (NVIR,), jnp.float32, 0.1, 3.0), 0.1, 3.0),
        "frequency": jnp.clip(jax.random.uniform(splits[5], (1,), jnp.float32, 0.3, 2.0), 0.3, 2.0),
    }


def reference(three_index, occ_index, vir_index, occ_energy, vir_energy, frequency):
    gap = jnp.take(vir_energy, vir_index) - jnp.take(occ_energy, occ_index)
    denominator = -4.0 * gap / (gap * gap + frequency[0] * frequency[0])
    scaled = (three_index.astype(jnp.float32) * denominator[None, :]).astype(jnp.bfloat16)
    matrix = lax.dot_general(scaled, three_index, (((1,), (1,)), ((), ())), preferred_element_type=jnp.float32)
    return matrix.reshape(NAUX, N_ROW, N_COL, AUX_DEV)
```

```python
import jax
import jax.numpy as jnp
from jax import lax
from jax.experimental import pallas as pl
from jax.experimental.pallas import tpu as pltpu
from jax.sharding import PartitionSpec as P

NT = (((1,), (1,)), ((), ()))
LANES = 128
N_ROW, N_COL = 8, 16
FIRST = 96


def z_ring():
    pairs = []
    for r in range(N_ROW):
        for c in range(N_COL):
            z = (r % 4 + (1 if c % 2 == 0 else -1)) % 4
            pairs.append((r * N_COL + c, (r // 4 * 4 + z) * N_COL + c))
    return pairs


def other_x():
    return [(r, (r + 4) % N_ROW) for r in range(N_ROW)]


def scale(three_index, occ_index, vir_index, occ_energy, vir_energy, frequency, cuts):
    rows, pairs = three_index.shape
    chunks = pairs // LANES

    def table(energy):
        padded = -(-energy.shape[0] // (8 * LANES)) * 8 * LANES
        return jnp.pad(energy, (0, padded - energy.shape[0])).reshape(-1, LANES)

    def kernel(freq, occ, vir, occ_table, vir_table, b, *outs):
        def look_up(table_ref, index):
            high, low = index >> 7, index & (LANES - 1)
            found = jnp.zeros(index.shape, jnp.float32)
            for k in range(table_ref.shape[0]):
                line = jnp.broadcast_to(table_ref[k : k + 1, :], index.shape)
                found = jnp.where(high == k, jnp.take_along_axis(line, low, axis=1), found)
            return found

        gap = look_up(vir_table, vir[...]) - look_up(occ_table, occ[...])
        denominator = -4.0 * gap / (gap * gap + freq[0] * freq[0])
        for k in range(chunks):
            at = slice(k * LANES, (k + 1) * LANES)
            scaled = (b[:, at].astype(jnp.float32) * denominator[k : k + 1, :]).astype(jnp.bfloat16)
            start = 0
            for out in outs:
                out[:, at] = scaled[start : start + out.shape[0]]
                start += out.shape[0]

    vmem = pl.BlockSpec(memory_space=pltpu.VMEM)
    return pl.pallas_call(
        kernel,
        out_shape=[jax.ShapeDtypeStruct((n, pairs), jnp.bfloat16) for n in cuts],
        in_specs=[pl.BlockSpec(memory_space=pltpu.SMEM)] + [vmem] * 5,
        out_specs=[vmem] * len(cuts),
        compiler_params=pltpu.CompilerParams(vmem_limit_bytes=32 << 20),
    )(
        frequency,
        occ_index.reshape(chunks, LANES),
        vir_index.reshape(chunks, LANES),
        table(occ_energy),
        table(vir_energy),
        three_index,
    )


def multiply(a, pieces, places, out, offset, group):
    r = a.shape[0] // N_COL
    depth = a.shape[1]
    m = group * r
    tiles = N_COL // group
    n_pieces = len(pieces)
    pr = pieces[0].shape[0]
    width = 2 * LANES
    n_wide = N_ROW * LANES // width

    def kernel(*refs):
        place = refs[0]
        a_ref, j_refs = refs[1], refs[2 : 2 + n_pieces]
        o, j_all, a_buf, acc, j_sem, a_sem, o_sem = refs[-7:]
        loads = []
        for j in range(n_pieces):
            to = pl.multiple_of(place[j], pr)
            loads.append(pltpu.make_async_copy(j_refs[j], j_all.at[pl.ds(to, pr)], j_sem.at[j]))
            loads[-1].start()

        def load(t):
            return pltpu.make_async_copy(a_ref.at[pl.ds(t * m, m)], a_buf.at[t % 2], a_sem.at[t % 2])

        load(0).start()
        for c in loads:
            c.wait()
        pending = [[], []]
        for t in range(tiles):
            load(t).wait()
            if t + 1 < tiles:
                load(t + 1).start()
            for w in range(n_wide):
                slot = (t * n_wide + w) % 2
                for c in pending[slot]:
                    c.wait()
                tile = lax.dot_general(
                    a_buf[t % 2], j_all[w * width : (w + 1) * width, :], NT, preferred_element_type=jnp.float32
                )
                acc[slot] = tile.reshape(group, r, width)
                pending[slot] = []
                for h in range(2):
                    c = pltpu.make_async_copy(
                        acc.at[slot, :, :, h * LANES : (h + 1) * LANES],
                        o.at[t * group : (t + 1) * group, offset : offset + r, 2 * w + h, 0, :],
                        o_sem.at[slot, h],
                    )
                    c.start()
                    pending[slot].append(c)
        for p in pending:
            for c in p:
                c.wait()

    hbm = pl.BlockSpec(memory_space=pl.ANY)
    has = out is not None
    return pl.pallas_call(
        kernel,
        out_shape=jax.ShapeDtypeStruct((N_COL, LANES, N_ROW, 1, LANES), jnp.float32),
        in_specs=[pl.BlockSpec(memory_space=pltpu.SMEM)] + [hbm] * (1 + n_pieces + has),
        out_specs=hbm,
        input_output_aliases={2 + n_pieces: 0} if has else {},
        scratch_shapes=[
            pltpu.VMEM((N_ROW * LANES, depth), jnp.bfloat16),
            pltpu.VMEM((2, m, depth), jnp.bfloat16),
            pltpu.VMEM((2, group, r, width), jnp.float32),
            pltpu.SemaphoreType.DMA((n_pieces,)),
            pltpu.SemaphoreType.DMA((2,)),
            pltpu.SemaphoreType.DMA((2, 2)),
        ],
        compiler_params=pltpu.CompilerParams(vmem_limit_bytes=40 << 20),
        cost_estimate=pl.CostEstimate(
            flops=2 * a.shape[0] * N_ROW * LANES * depth, bytes_accessed=24 << 20, transcendentals=0
        ),
    )(places, a, *pieces, *([out] if has else []))


def after(value, *earlier):
    return lax.optimization_barrier((value,) + earlier)[0]


def shards(three_index, occ_index, vir_index, occ_energy, vir_energy, frequency):
    own = three_index.shape[0]
    cuts = (FIRST, own - FIRST)
    scaled = scale(three_index, occ_index, vir_index, occ_energy, vir_energy, frequency, cuts)
    first = lax.all_gather(scaled[0], "col", axis=0, tiled=True)
    second = lax.all_gather(scaled[1], "col", axis=0, tiled=True)

    ring = z_ring()
    half = own // 2
    mine = [three_index[:half], three_index[half:]]
    step = lambda block: lax.ppermute(block, ("row", "col"), ring)
    quarter = half // 2
    cross = [lax.ppermute(mine[0], "row", other_x())]
    for p in range(2):
        part = three_index[half + p * quarter : half + (p + 1) * quarter]
        cross.append(lax.ppermute(after(part, cross[-1]), "row", other_x()))
    near = [[m] for m in mine]
    for h in range(2):
        for _ in range(3):
            near[h].append(step(near[h][-1]))
    far = [[after(cross[0], near[0][3])], [after(jnp.concatenate(cross[1:], 0), near[1][3])]]
    for h in range(2):
        for _ in range(3):
            far[h].append(step(far[h][-1]))

    row, core = lax.axis_index("row"), lax.axis_index("col") % 2
    x_hi, z = row // 4, row % 4
    toward = 1 - 2 * core
    pieces, places = [], []
    for h in range(2):
        for i in range(4):
            for blocks, x in ((near, x_hi), (far, 1 - x_hi)):
                pieces.append(blocks[h][i])
                places.append((x * 4 + (z - i * toward) % 4) * own + h * half)
    places = jnp.stack(places).astype(jnp.int32)
    out = multiply(first, pieces, places, None, 0, 4)
    out = multiply(second, pieces, places, out, FIRST, 16)
    return out.reshape(N_COL * own, N_ROW, 1, own)


def solution(mesh):
    placed = (P(("row", "col"), None), P(), P(), P(), P(), P())
    return jax.shard_map(
        shards, mesh=mesh, in_specs=placed, out_specs=P("row", None, "col", None), check_vma=False
    )
```

```python
import jax
import jax.numpy as jnp
from jax import lax
from jax.experimental import pallas as pl
from jax.experimental.pallas import tpu as pltpu
from jax.sharding import PartitionSpec as P

NT = (((1,), (1,)), ((), ()))
LANES = 128
N_ROW, N_COL = 8, 16
PIECE = 64
VMEM = 60 << 20


def permutations():
    y_ring, z_ring = [], []
    for c in range(N_COL):
        way = 1 if c % 2 == 0 else -1
        y_ring.append((c, c // 8 * 8 + (c // 2 % 4 + way) % 4 * 2 + c % 2))
        for r in range(N_ROW):
            z_ring.append((r * N_COL + c, (r // 4 * 4 + (r % 4 + way) % 4) * N_COL + c))
    return {
        "y": ("col", y_ring),
        "z": (("row", "col"), z_ring),
        "x_lo": ("col", [(c, c ^ 8) for c in range(N_COL)]),
        "x_hi": ("row", [(r, r ^ 4) for r in range(N_ROW)]),
        "core": ("col", [(c, c ^ 1) for c in range(N_COL)]),
    }


PERMUTATIONS = permutations()


def send(kind, block, *earlier):
    axis, pairs = PERMUTATIONS[kind]
    return lax.ppermute(after(block, *earlier), axis, pairs)


def after(value, *earlier):
    return lax.optimization_barrier((value,) + earlier)[0] if earlier else value


def scale(three_index, occ_index, vir_index, occ_energy, vir_energy, frequency):
    rows, pairs = three_index.shape
    chunks = pairs // LANES

    def table(energy):
        padded = -(-energy.shape[0] // (8 * LANES)) * 8 * LANES
        return jnp.pad(energy, (0, padded - energy.shape[0])).reshape(-1, LANES)

    def kernel(freq, occ, vir, occ_table, vir_table, b, *outs):
        def look_up(table_ref, index):
            high, low = index >> 7, index & (LANES - 1)
            found = jnp.zeros(index.shape, jnp.float32)
            for k in range(table_ref.shape[0]):
                line = jnp.broadcast_to(table_ref[k : k + 1, :], index.shape)
                found = jnp.where(high == k, jnp.take_along_axis(line, low, axis=1), found)
            return found

        gap = look_up(vir_table, vir[...]) - look_up(occ_table, occ[...])
        denominator = -4.0 * gap / (gap * gap + freq[0] * freq[0])
        for k in range(chunks):
            at = slice(k * LANES, (k + 1) * LANES)
            scaled = (b[:, at].astype(jnp.float32) * denominator[k : k + 1, :]).astype(jnp.bfloat16)
            for h, out in enumerate(outs):
                out[:, at] = scaled[h * PIECE : (h + 1) * PIECE]

    vmem = pl.BlockSpec(memory_space=pltpu.VMEM)
    return pl.pallas_call(
        kernel,
        out_shape=[jax.ShapeDtypeStruct((PIECE, pairs), jnp.bfloat16)] * 2,
        in_specs=[pl.BlockSpec(memory_space=pltpu.SMEM)] + [vmem] * 5,
        out_specs=[vmem] * 2,
        compiler_params=pltpu.CompilerParams(vmem_limit_bytes=32 << 20),
    )(
        frequency,
        occ_index.reshape(chunks, LANES),
        vir_index.reshape(chunks, LANES),
        table(occ_energy),
        table(vir_energy),
        three_index,
    )


def multiply(a_parts, a_rows, j_groups, out):
    depth = a_parts[0].shape[1]
    pieces = [(p, t) for p, part in enumerate(a_parts) for t in range(part.shape[0] // PIECE)]
    tiles = [pieces[i : i + 8] for i in range(0, len(pieces), 8)]
    sizes = [len(g[1]) for g in j_groups]
    n_a, n_j, n_g = len(a_parts), sum(sizes), len(j_groups)
    width = 4 * LANES
    numbers = jnp.stack(list(a_rows) + [x for g in j_groups for x in g[2]] + [g[0] for g in j_groups]).astype(jnp.int32)
    has = out is not None

    def kernel(number, *refs):
        a_refs, j_refs = refs[:n_a], refs[n_a : n_a + n_j]
        o, j_all, a_buf, acc, j_sem, a_sem, o_sem = refs[-7:]
        j_loads = []
        for g in range(n_g):
            first = sum(sizes[:g])
            loads = []
            for j in range(first, first + sizes[g]):
                to = pl.multiple_of(number[len(pieces) + j], PIECE)
                n = j_refs[j].shape[0]
                loads.append(pltpu.make_async_copy(j_refs[j], j_all.at[g, pl.ds(to, n)], j_sem.at[j]))
            j_loads.append(loads)

        def a_load(t):
            return [
                pltpu.make_async_copy(
                    a_refs[p].at[pl.ds(s * PIECE, PIECE)], a_buf.at[t % 2, pl.ds(i * PIECE, PIECE)], a_sem.at[t % 2, i]
                )
                for i, (p, s) in enumerate(tiles[t])
            ]

        for c in j_loads[0] + a_load(0) + sum(j_loads[1:], []):
            c.start()
        pending = [[], []]
        step = 0
        for t, tile in enumerate(tiles):
            for c in a_load(t):
                c.wait()
            if t + 1 < len(tiles):
                for c in a_load(t + 1):
                    c.start()
            m = len(tile) * PIECE
            for g in range(n_g):
                if t == 0:
                    for c in j_loads[g]:
                        c.wait()
                slot = step % 2
                step += 1
                for c in pending[slot]:
                    c.wait()
                for w in range(2):
                    product = lax.dot_general(
                        a_buf[t % 2, :m], j_all[g, w * 256 : (w + 1) * 256, :], NT, preferred_element_type=jnp.float32
                    )
                    acc[slot, :m, 2 * w : 2 * w + 2, :] = product.reshape(m, 2, LANES)
                half = number[len(pieces) + n_j + g]
                pending[slot] = []
                for i in range(len(tile)):
                    to = pl.multiple_of(number[t * 8 + i], PIECE)
                    c = pltpu.make_async_copy(
                        acc.at[slot, pl.ds(i * PIECE, PIECE)], o.at[pl.ds(to, PIECE), half], o_sem.at[slot, i]
                    )
                    c.start()
                    pending[slot].append(c)
        for p in pending:
            for c in p:
                c.wait()

    hbm = pl.BlockSpec(memory_space=pl.ANY)
    return pl.pallas_call(
        kernel,
        out_shape=jax.ShapeDtypeStruct((N_COL * LANES, 2, 4, LANES), jnp.float32),
        in_specs=[pl.BlockSpec(memory_space=pltpu.SMEM)] + [hbm] * (n_a + n_j + has),
        out_specs=hbm,
        input_output_aliases={1 + n_a + n_j: 0} if has else {},
        scratch_shapes=[
            pltpu.VMEM((n_g, width, depth), jnp.bfloat16),
            pltpu.VMEM((2, 8 * PIECE, depth), jnp.bfloat16),
            pltpu.VMEM((2, 8 * PIECE, 4, LANES), jnp.float32),
            pltpu.SemaphoreType.DMA((n_j,)),
            pltpu.SemaphoreType.DMA((2, 8)),
            pltpu.SemaphoreType.DMA((2, 8)),
        ],
        compiler_params=pltpu.CompilerParams(vmem_limit_bytes=VMEM),
        cost_estimate=pl.CostEstimate(
            flops=2 * len(pieces) * PIECE * n_g * width * depth, bytes_accessed=16 << 20, transcendentals=0
        ),
    )(numbers, *a_parts, *[x for g in j_groups for x in g[1]], *([out] if has else []))


def shards(three_index, occ_index, vir_index, occ_energy, vir_energy, frequency):
    raw = [three_index[:PIECE], three_index[PIECE:]]
    scaled = scale(three_index, occ_index, vir_index, occ_energy, vir_energy, frequency)
    two = range(2)

    a_far, j_far = [send("x_lo", scaled[0])], [send("x_hi", raw[0])]
    a_far.append(send("x_lo", scaled[1], a_far[0]))
    j_far.append(send("x_hi", raw[1], j_far[0]))
    a = [[scaled[h]] for h in two]
    j = [[raw[h]] for h in two]
    for _ in range(3):
        for h in two:
            a[h].append(send("y", a[h][-1]))
            j[h].append(send("z", j[h][-1]))
    near_done = [a[h][3] for h in two] + [j[h][3] for h in two]
    an, jn = [], []
    for h in two:
        x, v, *_ = lax.optimization_barrier((a_far[h], j_far[h], a[h][3], j[h][3]))
        an.append([x])
        jn.append([v])
    for _ in range(3):
        for h in two:
            an[h].append(send("y", an[h][-1]))
            jn[h].append(send("z", jn[h][-1]))

    flat = lambda blocks, steps: [blocks[h][i] for i in steps for h in two]
    a_near, an_most, an_last = flat(a, range(4)), flat(an, range(3)), flat(an, [3])
    near_other = send("core", jnp.concatenate(a_near, 0), *near_done)
    most_other = send("core", jnp.concatenate(an_most, 0), jn[0][2], jn[1][2])
    last_other = send("core", jnp.concatenate(an_last, 0), jn[0][3], jn[1][3])

    row, col = lax.axis_index("row"), lax.axis_index("col")
    x_hi, z, x_lo, y, core = row // 4, row % 4, col // 8, col // 2 % 4, col % 2
    way = 1 - 2 * core

    def rows(x, other, steps):
        k, w = (1 - core, -way) if other else (core, way)
        return [((x * 4 + (y - i * w) % 4) * 2 + k) * LANES + h * PIECE for i in steps for h in two]

    places = [(z - i * way) % 4 * LANES + h * PIECE for i in range(4) for h in two]
    j_near = (x_hi, flat(j, range(4)), places)
    j_rest = (1 - x_hi, flat(jn, range(4)), places)
    near = (a_near + [near_other], rows(x_lo, 0, range(4)) + rows(x_lo, 1, range(4)))
    most = (an_most + [most_other], rows(1 - x_lo, 0, range(3)) + rows(1 - x_lo, 1, range(3)))
    last = (an_last + [last_other], rows(1 - x_lo, 0, [3]) + rows(1 - x_lo, 1, [3]))
    out = multiply(*near, [j_near], None)
    out = multiply(*most, [j_near], out)
    out = multiply(near[0] + most[0], near[1] + most[1], [j_rest], out)
    out = multiply(*last, [j_near, j_rest], out)
    return out.reshape(N_COL * LANES, N_ROW, 1, LANES)


def solution(mesh):
    placed = (P(("row", "col"), None), P(), P(), P(), P(), P())
    return jax.shard_map(
        shards, mesh=mesh, in_specs=placed, out_specs=P("row", None, "col", None), check_vma=False
    )
```

```python
import jax
import jax.numpy as jnp
from jax import lax
from jax.experimental import pallas as pl
from jax.experimental.pallas import tpu as pltpu
from jax.sharding import PartitionSpec as P

NT = (((1,), (1,)), ((), ()))
LANES = 128
N_ROW, N_COL = 8, 16
PIECE = 64
VMEM = 60 << 20


def permutations():
    y_ring, z_ring = [], []
    for c in range(N_COL):
        way = 1 if c % 2 == 0 else -1
        y_ring.append((c, c // 8 * 8 + (c // 2 % 4 + way) % 4 * 2 + c % 2))
        for r in range(N_ROW):
            z_ring.append((r * N_COL + c, (r // 4 * 4 + (r % 4 + way) % 4) * N_COL + c))
    return {
        "y": ("col", y_ring),
        "z": (("row", "col"), z_ring),
        "x_lo": ("col", [(c, c ^ 8) for c in range(N_COL)]),
        "x_hi": ("row", [(r, r ^ 4) for r in range(N_ROW)]),
        "core": ("col", [(c, c ^ 1) for c in range(N_COL)]),
    }


PERMUTATIONS = permutations()


def send(kind, block, *earlier):
    axis, pairs = PERMUTATIONS[kind]
    return lax.ppermute(after(block, *earlier), axis, pairs)


def after(value, *earlier):
    return lax.optimization_barrier((value,) + earlier)[0] if earlier else value


def scale(three_index, occ_index, vir_index, occ_energy, vir_energy, frequency):
    rows, pairs = three_index.shape
    chunks = pairs // LANES

    def table(energy):
        padded = -(-energy.shape[0] // (8 * LANES)) * 8 * LANES
        return jnp.pad(energy, (0, padded - energy.shape[0])).reshape(-1, LANES)

    def kernel(freq, occ, vir, occ_table, vir_table, b, *outs):
        def look_up(table_ref, index):
            high, low = index >> 7, index & (LANES - 1)
            found = jnp.zeros(index.shape, jnp.float32)
            for k in range(table_ref.shape[0]):
                line = jnp.broadcast_to(table_ref[k : k + 1, :], index.shape)
                found = jnp.where(high == k, jnp.take_along_axis(line, low, axis=1), found)
            return found

        gap = look_up(vir_table, vir[...]) - look_up(occ_table, occ[...])
        denominator = -4.0 * gap / (gap * gap + freq[0] * freq[0])
        for k in range(chunks):
            at = slice(k * LANES, (k + 1) * LANES)
            scaled = (b[:, at].astype(jnp.float32) * denominator[k : k + 1, :]).astype(jnp.bfloat16)
            for h, out in enumerate(outs):
                out[:, at] = scaled[h * PIECE : (h + 1) * PIECE]

    vmem = pl.BlockSpec(memory_space=pltpu.VMEM)
    return pl.pallas_call(
        kernel,
        out_shape=[jax.ShapeDtypeStruct((PIECE, pairs), jnp.bfloat16)] * 2,
        in_specs=[pl.BlockSpec(memory_space=pltpu.SMEM)] + [vmem] * 5,
        out_specs=[vmem] * 2,
        compiler_params=pltpu.CompilerParams(vmem_limit_bytes=32 << 20),
    )(
        frequency,
        occ_index.reshape(chunks, LANES),
        vir_index.reshape(chunks, LANES),
        table(occ_energy),
        table(vir_energy),
        three_index,
    )


def multiply(numbers, a_parts, a_rows, j_groups, out):
    depth = a_parts[0].shape[1]
    pieces = [(p, t) for p, part in enumerate(a_parts) for t in range(part.shape[0] // PIECE)]
    tiles = [pieces[i : i + 8] for i in range(0, len(pieces), 8)]
    sizes = [len(g[1]) for g in j_groups]
    n_a, n_j, n_g = len(a_parts), sum(sizes), len(j_groups)
    width = 4 * LANES
    j_places = [x for g in j_groups for x in g[2]]
    has = out is not None

    def kernel(number, *refs):
        a_refs, j_refs = refs[:n_a], refs[n_a : n_a + n_j]
        o, j_all, a_buf, acc, j_sem, a_sem, o_sem = refs[-7:]
        j_loads = []
        for g in range(n_g):
            first = sum(sizes[:g])
            loads = []
            for j in range(first, first + sizes[g]):
                to = pl.multiple_of(number[j_places[j]], PIECE)
                n = j_refs[j].shape[0]
                loads.append(pltpu.make_async_copy(j_refs[j], j_all.at[g, pl.ds(to, n)], j_sem.at[j]))
            j_loads.append(loads)

        def a_load(t):
            return [
                pltpu.make_async_copy(
                    a_refs[p].at[pl.ds(s * PIECE, PIECE)], a_buf.at[t % 2, pl.ds(i * PIECE, PIECE)], a_sem.at[t % 2, i]
                )
                for i, (p, s) in enumerate(tiles[t])
            ]

        for c in j_loads[0] + a_load(0):
            c.start()
        pending = [[], []]
        step = 0
        for t, tile in enumerate(tiles):
            for c in a_load(t):
                c.wait()
            if t == 0:
                for c in j_loads[0]:
                    c.wait()
                for c in sum(j_loads[1:], []):
                    c.start()
            if t + 1 < len(tiles):
                for c in a_load(t + 1):
                    c.start()
            m = len(tile) * PIECE
            for g in range(n_g):
                if t == 0 and g > 0:
                    for c in j_loads[g]:
                        c.wait()
                slot = step % 2
                step += 1
                for c in pending[slot]:
                    c.wait()
                for w in range(m // 256):
                    at = slice(w * 256, (w + 1) * 256)
                    product = lax.dot_general(a_buf[t % 2, at], j_all[g], NT, preferred_element_type=jnp.float32)
                    acc[slot, at] = product.reshape(256, 4, LANES)
                half = number[j_groups[g][0]]
                pending[slot] = []
                for i in range(len(tile)):
                    to = pl.multiple_of(number[a_rows[t * 8 + i]], PIECE)
                    c = pltpu.make_async_copy(
                        acc.at[slot, pl.ds(i * PIECE, PIECE)], o.at[pl.ds(to, PIECE), half], o_sem.at[slot, i]
                    )
                    c.start()
                    pending[slot].append(c)
        for p in pending:
            for c in p:
                c.wait()

    hbm = pl.BlockSpec(memory_space=pl.ANY)
    return pl.pallas_call(
        kernel,
        out_shape=jax.ShapeDtypeStruct((N_COL * LANES, 2, 4, LANES), jnp.float32),
        in_specs=[pl.BlockSpec(memory_space=pltpu.SMEM)] + [hbm] * (n_a + n_j + has),
        out_specs=hbm,
        input_output_aliases={1 + n_a + n_j: 0} if has else {},
        scratch_shapes=[
            pltpu.VMEM((n_g, width, depth), jnp.bfloat16),
            pltpu.VMEM((2, 8 * PIECE, depth), jnp.bfloat16),
            pltpu.VMEM((2, 8 * PIECE, 4, LANES), jnp.float32),
            pltpu.SemaphoreType.DMA((n_j,)),
            pltpu.SemaphoreType.DMA((2, 8)),
            pltpu.SemaphoreType.DMA((2, 8)),
        ],
        compiler_params=pltpu.CompilerParams(vmem_limit_bytes=VMEM),
        cost_estimate=pl.CostEstimate(
            flops=2 * len(pieces) * PIECE * n_g * width * depth, bytes_accessed=16 << 20, transcendentals=0
        ),
    )(numbers, *a_parts, *[x for g in j_groups for x in g[1]], *([out] if has else []))


def shards(three_index, occ_index, vir_index, occ_energy, vir_energy, frequency):
    raw = [three_index[:PIECE], three_index[PIECE:]]
    scaled = scale(three_index, occ_index, vir_index, occ_energy, vir_energy, frequency)
    two = range(2)
    flat = lambda blocks, steps: [blocks[h][i] for i in steps for h in two]

    row, col = lax.axis_index("row"), lax.axis_index("col")
    x_hi, z, x_lo, y, core = row // 4, row % 4, col // 8, col // 2 % 4, col % 2
    way = 1 - 2 * core
    numbers, at = [], {}
    for x in two:
        for other in two:
            k, w = (1 - core, -way) if other else (core, way)
            for i in range(4):
                for h in two:
                    at["row", x, other, i, h] = len(numbers)
                    numbers.append((((x_lo ^ x) * 4 + (y - i * w) % 4) * 2 + k) * LANES + h * PIECE)
    for i in range(4):
        for h in two:
            at["place", i, h] = len(numbers)
            numbers.append((z - i * way) % 4 * LANES + h * PIECE)
    at["half", 0], at["half", 1] = len(numbers), len(numbers) + 1
    numbers = jnp.stack(numbers + [x_hi, 1 - x_hi]).astype(jnp.int32)
    rows = lambda x, other, steps: [at["row", x, other, i, h] for i in steps for h in two]
    columns = lambda x, blocks: (at["half", x], flat(blocks, range(4)), [at["place", i, h] for i in range(4) for h in two])

    a_far, j_far = [send("x_lo", scaled[0])], [send("x_hi", raw[0])]
    a_far.append(send("x_lo", scaled[1], a_far[0]))
    j_far.append(send("x_hi", raw[1], j_far[0]))
    a = [[scaled[h]] for h in two]
    j = [[raw[h]] for h in two]
    for _ in range(3):
        for h in two:
            a[h].append(send("y", a[h][-1]))
            j[h].append(send("z", j[h][-1]))
    near_done = [a[h][3] for h in two] + [j[h][3] for h in two]
    near = flat(a, range(4))
    near_other = send("core", jnp.concatenate(near, 0), *near_done)
    an, jn = [], []
    for h in two:
        x, v, *_ = lax.optimization_barrier((a_far[h], j_far[h], a[h][3], j[h][3]))
        an.append([x])
        jn.append([v])
    for _ in range(3):
        for h in two:
            an[h].append(send("y", an[h][-1]))
            jn[h].append(send("z", jn[h][-1]))
    rest = flat(an, range(4))
    rest_other = send("core", jnp.concatenate(rest, 0), jn[0][3], jn[1][3])
    both = [columns(0, j), columns(1, jn)]
    out = multiply(
        numbers,
        near + [near_other] + rest,
        rows(0, 0, range(4)) + rows(0, 1, range(4)) + rows(1, 0, range(4)),
        both,
        None,
    )
    out = multiply(numbers, [rest_other], rows(1, 1, range(4)), both, out)
    return out.reshape(N_COL * LANES, N_ROW, 1, LANES)


def solution(mesh):
    placed = (P(("row", "col"), None), P(), P(), P(), P(), P())
    return jax.shard_map(
        shards, mesh=mesh, in_specs=placed, out_specs=P("row", None, "col", None), check_vma=False
    )
```

```python
import jax
import jax.numpy as jnp
from jax import lax
from jax.experimental import pallas as pl
from jax.experimental.pallas import tpu as pltpu
from jax.sharding import PartitionSpec as P

NT = (((1,), (1,)), ((), ()))
LANES = 128
N_ROW, N_COL = 8, 16
PIECE = 64
VMEM = 60 << 20


def permutations():
    y_ring, z_ring = [], []
    for c in range(N_COL):
        way = 1 if c % 2 == 0 else -1
        y_ring.append((c, c // 8 * 8 + (c // 2 % 4 + way) % 4 * 2 + c % 2))
        for r in range(N_ROW):
            z_ring.append((r * N_COL + c, (r // 4 * 4 + (r % 4 + way) % 4) * N_COL + c))
    return {
        "y": ("col", y_ring),
        "z": (("row", "col"), z_ring),
        "x_lo": ("col", [(c, c ^ 8) for c in range(N_COL)]),
        "x_hi": ("row", [(r, r ^ 4) for r in range(N_ROW)]),
        "core": ("col", [(c, c ^ 1) for c in range(N_COL)]),
    }


PERMUTATIONS = permutations()


def send(kind, block, *earlier):
    axis, pairs = PERMUTATIONS[kind]
    return lax.ppermute(after(block, *earlier), axis, pairs)


def after(value, *earlier):
    return lax.optimization_barrier((value,) + earlier)[0] if earlier else value


def scale(three_index, occ_index, vir_index, occ_energy, vir_energy, frequency):
    rows, pairs = three_index.shape
    chunks = pairs // LANES
    lines = [-(-e.shape[0] // LANES) for e in (vir_energy, occ_energy)]

    def padded(energy):
        return jnp.pad(energy, (0, -energy.shape[0] % LANES))

    tables = jnp.concatenate([padded(vir_energy), padded(occ_energy)]).reshape(-1, LANES)

    def kernel(freq, *refs):
        sources, outs, buffers, sem = refs[:4], refs[4:6], refs[6:10], refs[10]
        loads = [pltpu.make_async_copy(s, d, sem.at[i]) for i, (s, d) in enumerate(zip(sources, buffers))]
        for c in loads:
            c.start()
        for c in loads[:3]:
            c.wait()
        occ, vir, table, b = buffers

        def look_up(first, count, index):
            high, low = index >> 7, index & (LANES - 1)
            found = jnp.zeros(index.shape, jnp.float32)
            for k in range(count):
                line = jnp.broadcast_to(table[first + k : first + k + 1, :], index.shape)
                found = jnp.where(high == k, jnp.take_along_axis(line, low, axis=1), found)
            return found

        gap = look_up(0, lines[0], vir[...]) - look_up(lines[0], lines[1], occ[...])
        denominator = -4.0 * gap / (gap * gap + freq[0] * freq[0])
        loads[3].wait()
        for k in range(chunks):
            at = slice(k * LANES, (k + 1) * LANES)
            scaled = (b[:, at].astype(jnp.float32) * denominator[k : k + 1, :]).astype(jnp.bfloat16)
            for h, out in enumerate(outs):
                out[:, at] = scaled[h * PIECE : (h + 1) * PIECE]

    vmem, hbm = pl.BlockSpec(memory_space=pltpu.VMEM), pl.BlockSpec(memory_space=pl.ANY)
    return pl.pallas_call(
        kernel,
        out_shape=[jax.ShapeDtypeStruct((PIECE, pairs), jnp.bfloat16)] * 2,
        in_specs=[pl.BlockSpec(memory_space=pltpu.SMEM)] + [hbm] * 4,
        out_specs=[vmem] * 2,
        scratch_shapes=[
            pltpu.VMEM((chunks, LANES), jnp.int32),
            pltpu.VMEM((chunks, LANES), jnp.int32),
            pltpu.VMEM((sum(lines), LANES), jnp.float32),
            pltpu.VMEM((rows, pairs), jnp.bfloat16),
            pltpu.SemaphoreType.DMA((4,)),
        ],
        compiler_params=pltpu.CompilerParams(vmem_limit_bytes=VMEM),
    )(frequency, occ_index.reshape(chunks, LANES), vir_index.reshape(chunks, LANES), tables, three_index)


def multiply(numbers, a_parts, a_rows, j_groups, out):
    depth = a_parts[0].shape[1]
    pieces = [(p, t) for p, part in enumerate(a_parts) for t in range(part.shape[0] // PIECE)]
    tiles = [pieces[i : i + 8] for i in range(0, len(pieces), 8)]
    sizes = [len(g[1]) for g in j_groups]
    n_a, n_j, n_g = len(a_parts), sum(sizes), len(j_groups)
    width = 4 * LANES
    j_places = [x for g in j_groups for x in g[2]]
    has = out is not None

    def kernel(number, *refs):
        a_refs, j_refs = refs[:n_a], refs[n_a : n_a + n_j]
        o, j_all, a_buf, acc, j_sem, a_sem, o_sem = refs[-7:]
        j_loads = []
        for g in range(n_g):
            first = sum(sizes[:g])
            loads = []
            for j in range(first, first + sizes[g]):
                to = pl.multiple_of(number[j_places[j]], PIECE)
                n = j_refs[j].shape[0]
                loads.append(pltpu.make_async_copy(j_refs[j], j_all.at[g, pl.ds(to, n)], j_sem.at[j]))
            j_loads.append(loads)

        def a_load(t):
            return [
                pltpu.make_async_copy(
                    a_refs[p].at[pl.ds(s * PIECE, PIECE)], a_buf.at[t % 2, pl.ds(i * PIECE, PIECE)], a_sem.at[t % 2, i]
                )
                for i, (p, s) in enumerate(tiles[t])
            ]

        for c in j_loads[0] + a_load(0):
            c.start()
        pending = [[], []]
        step = 0
        for t, tile in enumerate(tiles):
            for c in a_load(t):
                c.wait()
            if t == 0:
                for c in j_loads[0]:
                    c.wait()
                for c in sum(j_loads[1:], []):
                    c.start()
            if t + 1 < len(tiles):
                for c in a_load(t + 1):
                    c.start()
            m = len(tile) * PIECE
            for g in range(n_g):
                if t == 0 and g > 0:
                    for c in j_loads[g]:
                        c.wait()
                slot = step % 2
                step += 1
                for c in pending[slot]:
                    c.wait()
                for w in range(m // 256):
                    at = slice(w * 256, (w + 1) * 256)
                    product = lax.dot_general(a_buf[t % 2, at], j_all[g], NT, preferred_element_type=jnp.float32)
                    acc[slot, at] = product.reshape(256, 4, LANES)
                half = number[j_groups[g][0]]
                pending[slot] = []
                for i in range(len(tile)):
                    to = pl.multiple_of(number[a_rows[t * 8 + i]], PIECE)
                    c = pltpu.make_async_copy(
                        acc.at[slot, pl.ds(i * PIECE, PIECE)], o.at[pl.ds(to, PIECE), half], o_sem.at[slot, i]
                    )
                    c.start()
                    pending[slot].append(c)
        for p in pending:
            for c in p:
                c.wait()

    hbm = pl.BlockSpec(memory_space=pl.ANY)
    return pl.pallas_call(
        kernel,
        out_shape=jax.ShapeDtypeStruct((N_COL * LANES, 2, 4, LANES), jnp.float32),
        in_specs=[pl.BlockSpec(memory_space=pltpu.SMEM)] + [hbm] * (n_a + n_j + has),
        out_specs=hbm,
        input_output_aliases={1 + n_a + n_j: 0} if has else {},
        scratch_shapes=[
            pltpu.VMEM((n_g, width, depth), jnp.bfloat16),
            pltpu.VMEM((2, 8 * PIECE, depth), jnp.bfloat16),
            pltpu.VMEM((2, 8 * PIECE, 4, LANES), jnp.float32),
            pltpu.SemaphoreType.DMA((n_j,)),
            pltpu.SemaphoreType.DMA((2, 8)),
            pltpu.SemaphoreType.DMA((2, 8)),
        ],
        compiler_params=pltpu.CompilerParams(vmem_limit_bytes=VMEM),
        cost_estimate=pl.CostEstimate(
            flops=2 * len(pieces) * PIECE * n_g * width * depth, bytes_accessed=16 << 20, transcendentals=0
        ),
    )(numbers, *a_parts, *[x for g in j_groups for x in g[1]], *([out] if has else []))


def shards(three_index, occ_index, vir_index, occ_energy, vir_energy, frequency):
    raw = [three_index[:PIECE], three_index[PIECE:]]
    scaled = scale(three_index, occ_index, vir_index, occ_energy, vir_energy, frequency)
    two = range(2)
    flat = lambda blocks, steps: [blocks[h][i] for i in steps for h in two]

    row, col = lax.axis_index("row"), lax.axis_index("col")
    x_hi, z, x_lo, y, core = row // 4, row % 4, col // 8, col // 2 % 4, col % 2
    way = 1 - 2 * core
    numbers, at = [], {}
    for x in two:
        for other in two:
            k, w = (1 - core, -way) if other else (core, way)
            for i in range(4):
                for h in two:
                    at["row", x, other, i, h] = len(numbers)
                    numbers.append((((x_lo ^ x) * 4 + (y - i * w) % 4) * 2 + k) * LANES + h * PIECE)
    for i in range(4):
        for h in two:
            at["place", i, h] = len(numbers)
            numbers.append((z - i * way) % 4 * LANES + h * PIECE)
    at["half", 0], at["half", 1] = len(numbers), len(numbers) + 1
    numbers = jnp.stack(numbers + [x_hi, 1 - x_hi]).astype(jnp.int32)
    rows = lambda x, other, steps: [at["row", x, other, i, h] for i in steps for h in two]
    columns = lambda x, blocks: (at["half", x], flat(blocks, range(4)), [at["place", i, h] for i in range(4) for h in two])

    a_far, j_far = [send("x_lo", scaled[0])], [send("x_hi", raw[0])]
    a_far.append(send("x_lo", scaled[1], a_far[0]))
    j_far.append(send("x_hi", raw[1], j_far[0]))
    a = [[scaled[h]] for h in two]
    j = [[raw[h]] for h in two]
    for i in range(3):
        for h in two:
            crossed = [a_far[0], j_far[0]] if i == 2 else []
            x, v, *_ = lax.optimization_barrier((a[h][-1], j[h][-1], *crossed)) if i else (a[h][-1], j[h][-1])
            a[h].append(send("y", x))
            j[h].append(send("z", v))
    near_done = [a[h][3] for h in two] + [j[h][3] for h in two]
    near = flat(a, range(4))
    near_other = send("core", jnp.concatenate(near, 0), *near_done, numbers)
    an, jn = [], []
    for h in two:
        x, v, *_ = lax.optimization_barrier((a_far[h], j_far[h], a[h][3], j[h][3]))
        an.append([x])
        jn.append([v])
    for _ in range(3):
        for h in two:
            x, v = lax.optimization_barrier((an[h][-1], jn[h][-1]))
            an[h].append(send("y", x))
            jn[h].append(send("z", v))
    rest = flat(an, range(4))
    rest_other = send("core", jnp.concatenate(rest, 0), jn[0][3], jn[1][3])
    both = [columns(0, j), columns(1, jn)]
    out = multiply(
        numbers,
        near + [near_other] + rest,
        rows(0, 0, range(4)) + rows(0, 1, range(4)) + rows(1, 0, range(4)),
        both,
        None,
    )
    out = multiply(numbers, [rest_other], rows(1, 1, range(4)), both, out)
    return out.reshape(N_COL * LANES, N_ROW, 1, LANES)


def solution(mesh):
    placed = (P(("row", "col"), None), P(), P(), P(), P(), P())
    return jax.shard_map(
        shards, mesh=mesh, in_specs=placed, out_specs=P("row", None, "col", None), check_vma=False
    )
```

```python
import jax
import jax.numpy as jnp
from jax import lax
from jax.experimental import pallas as pl
from jax.experimental.pallas import tpu as pltpu
from jax.sharding import PartitionSpec as P

NT = (((1,), (1,)), ((), ()))
LANES = 128
N_ROW, N_COL = 8, 16
PIECE = 64
VMEM = 60 << 20


def permutations():
    y_ring, z_ring = [], []
    for c in range(N_COL):
        way = 1 if c % 2 == 0 else -1
        y_ring.append((c, c // 8 * 8 + (c // 2 % 4 + way) % 4 * 2 + c % 2))
        for r in range(N_ROW):
            z_ring.append((r * N_COL + c, (r // 4 * 4 + (r % 4 + way) % 4) * N_COL + c))
    return {
        "y": ("col", y_ring),
        "z": (("row", "col"), z_ring),
        "x_lo": ("col", [(c, c ^ 8) for c in range(N_COL)]),
        "x_hi": ("row", [(r, r ^ 4) for r in range(N_ROW)]),
        "core": ("col", [(c, c ^ 1) for c in range(N_COL)]),
    }


PERMUTATIONS = permutations()


def send(kind, block, *earlier):
    axis, pairs = PERMUTATIONS[kind]
    return lax.ppermute(after(block, *earlier), axis, pairs)


def after(value, *earlier):
    return lax.optimization_barrier((value,) + earlier)[0] if earlier else value


def scale(three_index, occ_index, vir_index, occ_energy, vir_energy, frequency):
    rows, pairs = three_index.shape
    chunks = pairs // LANES
    lines = [-(-e.shape[0] // LANES) for e in (vir_energy, occ_energy)]

    def padded(energy):
        return jnp.pad(energy, (0, -energy.shape[0] % LANES))

    tables = jnp.concatenate([padded(vir_energy), padded(occ_energy)]).reshape(-1, LANES)

    def kernel(freq, *refs):
        sources, outs, buffers, sem = refs[:4], refs[4:6], refs[6:10], refs[10]
        loads = [pltpu.make_async_copy(s, d, sem.at[i]) for i, (s, d) in enumerate(zip(sources, buffers))]
        for c in loads:
            c.start()
        for c in loads[:3]:
            c.wait()
        occ, vir, table, b = buffers

        def look_up(first, count, index):
            high, low = index >> 7, index & (LANES - 1)
            found = jnp.zeros(index.shape, jnp.float32)
            for k in range(count):
                line = jnp.broadcast_to(table[first + k : first + k + 1, :], index.shape)
                found = jnp.where(high == k, jnp.take_along_axis(line, low, axis=1), found)
            return found

        gap = look_up(0, lines[0], vir[...]) - look_up(lines[0], lines[1], occ[...])
        denominator = -4.0 * gap / (gap * gap + freq[0] * freq[0])
        loads[3].wait()
        for k in range(chunks):
            at = slice(k * LANES, (k + 1) * LANES)
            scaled = (b[:, at].astype(jnp.float32) * denominator[k : k + 1, :]).astype(jnp.bfloat16)
            for h, out in enumerate(outs):
                out[:, at] = scaled[h * PIECE : (h + 1) * PIECE]

    vmem, hbm = pl.BlockSpec(memory_space=pltpu.VMEM), pl.BlockSpec(memory_space=pl.ANY)
    return pl.pallas_call(
        kernel,
        out_shape=[jax.ShapeDtypeStruct((PIECE, pairs), jnp.bfloat16)] * 2,
        in_specs=[pl.BlockSpec(memory_space=pltpu.SMEM)] + [hbm] * 4,
        out_specs=[vmem] * 2,
        scratch_shapes=[
            pltpu.VMEM((chunks, LANES), jnp.int32),
            pltpu.VMEM((chunks, LANES), jnp.int32),
            pltpu.VMEM((sum(lines), LANES), jnp.float32),
            pltpu.VMEM((rows, pairs), jnp.bfloat16),
            pltpu.SemaphoreType.DMA((4,)),
        ],
        compiler_params=pltpu.CompilerParams(vmem_limit_bytes=VMEM),
    )(frequency, occ_index.reshape(chunks, LANES), vir_index.reshape(chunks, LANES), tables, three_index)


def multiply(numbers, a_parts, a_rows, j_groups, out):
    depth = a_parts[0].shape[1]
    pieces = [(p, t) for p, part in enumerate(a_parts) for t in range(part.shape[0] // PIECE)]
    tiles = [pieces[i : i + 8] for i in range(0, len(pieces), 8)]
    sizes = [len(g[1]) for g in j_groups]
    n_a, n_j, n_g = len(a_parts), sum(sizes), len(j_groups)
    width = 4 * LANES
    j_places = [x for g in j_groups for x in g[2]]
    has = out is not None

    def kernel(number, *refs):
        a_refs, j_refs = refs[:n_a], refs[n_a : n_a + n_j]
        o, j_all, a_buf, acc, j_sem, a_sem, o_sem = refs[-7:]
        j_loads = []
        for g in range(n_g):
            first = sum(sizes[:g])
            loads = []
            for j in range(first, first + sizes[g]):
                to = pl.multiple_of(number[j_places[j]], PIECE)
                n = j_refs[j].shape[0]
                loads.append(pltpu.make_async_copy(j_refs[j], j_all.at[g, pl.ds(to, n)], j_sem.at[j]))
            j_loads.append(loads)

        def a_load(t):
            return [
                pltpu.make_async_copy(
                    a_refs[p].at[pl.ds(s * PIECE, PIECE)], a_buf.at[t % 2, pl.ds(i * PIECE, PIECE)], a_sem.at[t % 2, i]
                )
                for i, (p, s) in enumerate(tiles[t])
            ]

        for c in j_loads[0] + a_load(0):
            c.start()
        pending = [[], []]
        step = 0
        for t, tile in enumerate(tiles):
            for c in a_load(t):
                c.wait()
            if t == 0:
                for c in j_loads[0]:
                    c.wait()
                for c in sum(j_loads[1:], []):
                    c.start()
            if t and t + 1 < len(tiles):
                for c in a_load(t + 1):
                    c.start()
            m = len(tile) * PIECE
            for g in range(n_g):
                if t == 0 and g > 0:
                    for c in j_loads[g]:
                        c.wait()
                    if g == n_g - 1 and len(tiles) > 1:
                        for c in a_load(1):
                            c.start()
                slot = step % 2
                step += 1
                for c in pending[slot]:
                    c.wait()
                for w in range(m // 256):
                    at = slice(w * 256, (w + 1) * 256)
                    product = lax.dot_general(a_buf[t % 2, at], j_all[g], NT, preferred_element_type=jnp.float32)
                    acc[slot, at] = product.reshape(256, 4, LANES)
                half = number[j_groups[g][0]]
                pending[slot] = []
                for i in range(len(tile)):
                    to = pl.multiple_of(number[a_rows[t * 8 + i]], PIECE)
                    c = pltpu.make_async_copy(
                        acc.at[slot, pl.ds(i * PIECE, PIECE)], o.at[pl.ds(to, PIECE), half], o_sem.at[slot, i]
                    )
                    c.start()
                    pending[slot].append(c)
        for p in pending:
            for c in p:
                c.wait()

    hbm = pl.BlockSpec(memory_space=pl.ANY)
    return pl.pallas_call(
        kernel,
        out_shape=jax.ShapeDtypeStruct((N_COL * LANES, 2, 4, LANES), jnp.float32),
        in_specs=[pl.BlockSpec(memory_space=pltpu.SMEM)] + [hbm] * (n_a + n_j + has),
        out_specs=hbm,
        input_output_aliases={1 + n_a + n_j: 0} if has else {},
        scratch_shapes=[
            pltpu.VMEM((n_g, width, depth), jnp.bfloat16),
            pltpu.VMEM((2, 8 * PIECE, depth), jnp.bfloat16),
            pltpu.VMEM((2, 8 * PIECE, 4, LANES), jnp.float32),
            pltpu.SemaphoreType.DMA((n_j,)),
            pltpu.SemaphoreType.DMA((2, 8)),
            pltpu.SemaphoreType.DMA((2, 8)),
        ],
        compiler_params=pltpu.CompilerParams(vmem_limit_bytes=VMEM),
        cost_estimate=pl.CostEstimate(
            flops=2 * len(pieces) * PIECE * n_g * width * depth, bytes_accessed=16 << 20, transcendentals=0
        ),
    )(numbers, *a_parts, *[x for g in j_groups for x in g[1]], *([out] if has else []))


def shards(three_index, occ_index, vir_index, occ_energy, vir_energy, frequency):
    raw = [three_index[:PIECE], three_index[PIECE:]]
    scaled = scale(three_index, occ_index, vir_index, occ_energy, vir_energy, frequency)
    two = range(2)
    flat = lambda blocks, steps: [blocks[h][i] for i in steps for h in two]

    row, col = lax.axis_index("row"), lax.axis_index("col")
    x_hi, z, x_lo, y, core = row // 4, row % 4, col // 8, col // 2 % 4, col % 2
    way = 1 - 2 * core
    numbers, at = [], {}
    for x in two:
        for other in two:
            k, w = (1 - core, -way) if other else (core, way)
            for i in range(4):
                for h in two:
                    at["row", x, other, i, h] = len(numbers)
                    numbers.append((((x_lo ^ x) * 4 + (y - i * w) % 4) * 2 + k) * LANES + h * PIECE)
    for i in range(4):
        for h in two:
            at["place", i, h] = len(numbers)
            numbers.append((z - i * way) % 4 * LANES + h * PIECE)
    at["half", 0], at["half", 1] = len(numbers), len(numbers) + 1
    numbers = jnp.stack(numbers + [x_hi, 1 - x_hi]).astype(jnp.int32)
    rows = lambda x, other, steps: [at["row", x, other, i, h] for i in steps for h in two]
    columns = lambda x, blocks: (at["half", x], flat(blocks, range(4)), [at["place", i, h] for i in range(4) for h in two])

    a_far, j_far = [send("x_lo", scaled[0])], [send("x_hi", raw[0])]
    a_far.append(send("x_lo", scaled[1], a_far[0]))
    j_far.append(send("x_hi", raw[1], j_far[0]))
    a = [[scaled[h]] for h in two]
    j = [[raw[h]] for h in two]
    for i in range(3):
        for h in two:
            crossed = [a_far[0], j_far[0]] if i == 2 else []
            x, v, *_ = lax.optimization_barrier((a[h][-1], j[h][-1], *crossed)) if i else (a[h][-1], j[h][-1])
            a[h].append(send("y", x))
            j[h].append(send("z", v))
    near_done = [a[h][3] for h in two] + [j[h][3] for h in two]
    near = flat(a, range(4))
    near_other = send("core", jnp.concatenate(near, 0), *near_done, numbers)
    an, jn = [], []
    for h in two:
        x, v, *_ = lax.optimization_barrier((a_far[h], j_far[h], a[h][3], j[h][3]))
        an.append([x])
        jn.append([v])
    for _ in range(3):
        for h in two:
            x, v = lax.optimization_barrier((an[h][-1], jn[h][-1]))
            an[h].append(send("y", x))
            jn[h].append(send("z", v))
    rest = flat(an, range(4))
    rest_other = send("core", jnp.concatenate(rest, 0), jn[0][3], jn[1][3])
    both = [columns(0, j), columns(1, jn)]
    out = multiply(
        numbers,
        near + [near_other] + rest,
        rows(0, 0, range(4)) + rows(0, 1, range(4)) + rows(1, 0, range(4)),
        both,
        None,
    )
    out = multiply(numbers, [rest_other], rows(1, 1, range(4)), both, out)
    return out.reshape(N_COL * LANES, N_ROW, 1, LANES)


def solution(mesh):
    placed = (P(("row", "col"), None), P(), P(), P(), P(), P())
    return jax.shard_map(
        shards, mesh=mesh, in_specs=placed, out_specs=P("row", None, "col", None), check_vma=False
    )
```
